32 devices in a mesh: gx: 16 (over z, y, core), gz: 2 (over x).
Axes of the slice: x: 2, y: 2, z: 4, core: 2. Of those that a mesh axis runs over, the one named last changes fastest.
Arguments:
- populations: float32 [19, 32, 16, 256], P(None, 'gx', None, 'gz'), as said below
- solid: int32 [32, 16, 256], P('gx', None, 'gz'), may hold values 0 or 1
- cell_index: int32 [65536], P(('gx', 'gz')), may hold values from 0 to 4095
- offset: float32 [65536], P(('gx', 'gz')), may hold values from 0 to 1
- velocity: float32 [3, 65536], P(None, ('gx', 'gz')), may hold values from -0.6 to 0.6
- mass: float32 [65536], P(('gx', 'gz')), may hold values from 0.2 to 2
- counts: int32 [16, 2], P('gx', 'gz'), may hold values from 512 to 2048, as said below
Outputs:
- new_populations: float32 [19, 32, 16, 256], P(None, 'gx', None, 'gz')
- new_velocity: float32 [3, 65536], P(None, ('gx', 'gz'))
The draws below stay inside these ranges and needn't reach their ends.
Inputs may be any that keep to these rules, and one draw needn't show every extreme that they name: `cell_index`: an index of a cell of the device's own block, numbered with z fastest, then y, then x. `counts`: some device has all 2048 slots live in every draw. Positive populations.
All inputs are finite; a program needn't handle non-finite values. No bound on the sum of `solid` on one device may be relied on, other than what follows from the above.
Results may differ from the reference program's by a relative error of at most 0.0001.
Values sent between devices are 32-bit elements; how exact they have to be, the bound alone decides.
A program may use at most 64 MiB of HBM per device.

```python
import math
import jax
import jax.numpy as jnp
import numpy as np

CX = 2
NY = 16
CZ = 128
P_CAP = 2048
SUBSTEPS = 2
NX = 32
NZ = 256
PARTS_SIZE = 65536
N_GX = 16
N_GZ = 2


LATTICE = np.array([[0, 0, 0], [1, 0, 0], [-1, 0, 0], [0, 1, 0], [0, -1, 0], [0, 0, 1], [0, 0, -1], [1, 1, 0], [-1, -1, 0], [1, -1, 0], [-1, 1, 0], [1, 0, 1], [-1, 0, -1], [1, 0, -1], [-1, 0, 1], [0, 1, 1], [0, -1, -1], [0, 1, -1], [0, -1, 1]])


WEIGHTS = [1.0 / 3.0] + [1.0 / 18.0] * 6 + [1.0 / 36.0] * 12


def draw_populations(key, part):
    key = jax.random.fold_in(key, 11)
    keys = jax.random.split(key, 3)
    shape = (CX * N_GX, NY, CZ * N_GZ)
    flow = jax.random.uniform(keys[0], (3,) + shape, jnp.float32, -0.08, 0.08)
    noise = jax.random.uniform(keys[1], (19,) + shape, jnp.float32, -0.2, 0.2)
    density = jax.random.uniform(keys[2], shape, jnp.float32, 0.9, 1.1)
    lattice = jnp.asarray(LATTICE, jnp.float32)
    along = lattice[:, 0, None, None, None] * flow[0] + lattice[:, 1, None, None, None] * flow[1] + lattice[:, 2, None, None, None] * flow[2]
    weights = jnp.asarray(WEIGHTS, jnp.float32)[:, None, None, None]
    return weights * density * (1.0 + 3.0 * along + noise)


def draw_counts(key, part):
    key = jax.random.fold_in(key, 23)
    keys = jax.random.split(key, 2)
    values = jax.random.randint(keys[0], (N_GX * N_GZ,), P_CAP // 4, P_CAP + 1)
    fullest = jax.random.randint(keys[1], (), 0, N_GX * N_GZ)
    values = values.at[fullest].set(P_CAP)
    return values.reshape(N_GX, N_GZ).astype(jnp.int32)


def plant(entries, rng, low, high):
    extent = entries.shape
    index_at = [jax.random.randint(jax.random.fold_in(rng, axis), (), 0, extent[axis]) for axis in range(len(extent))]
    entries = entries.at[tuple(index_at)].set(low)
    longest = extent.index(max(extent))
    index_at[longest] = (index_at[longest] + 1) % extent[longest]
    return entries.at[tuple(index_at)].set(high)


def levels(own_key, shape, pieces, least, high):
    level, own = 1.0, jax.random.fold_in(own_key, 6)
    for axis_at, blocks in pieces:
        draws = jnp.exp(jax.random.uniform(jax.random.fold_in(own, axis_at), (blocks,), jnp.float32, least / len(pieces), high / len(pieces)))
        level = level * jnp.repeat(draws, shape[axis_at] // blocks).reshape([-1 if axis == axis_at else 1 for axis in range(len(shape))])
    return level


def normal_values(rng, dims, width, bound, shards=(), kind=jnp.bfloat16):
    values = width * jax.random.normal(rng, dims, jnp.float32)
    if shards:
        values = values * levels(rng, dims, shards, -0.22, 0.18)
    return jnp.clip(values, -bound, bound).astype(kind)


def setup_inputs(seed: int = 0) -> dict:
    arg_keys = jax.random.split(jax.random.key(seed), 8)
    populations = draw_populations(jax.random.fold_in(arg_keys[7], 71), 0)
    solid = plant((jax.random.randint(arg_keys[1], (NX, NY, NZ), 0, 10) < 1).astype(jnp.int32), jax.random.fold_in(arg_keys[1], 1), 0, 1)
    cell_index = plant(jax.random.randint(arg_keys[2], (PARTS_SIZE,), 0, CX * NY * CZ), jax.random.fold_in(arg_keys[2], 1), 0, (CX * NY * CZ) - 1).astype(jnp.int32)
    offset = jnp.clip(1.0 * jax.random.uniform(arg_keys[3], (PARTS_SIZE,), jnp.float32) ** levels(arg_keys[3], (PARTS_SIZE,), ((0, 32),), -0.2, 0.2), 0.0, 1.0)
    velocity = normal_values(arg_keys[4], (3, PARTS_SIZE), 0.1, 0.6, ((1, 32),), jnp.float32)
    mass = jnp.clip(jnp.exp(math.log(2.0) - 2.3025851 * jax.random.uniform(arg_keys[5], (PARTS_SIZE,), jnp.float32) ** levels(arg_keys[5], (PARTS_SIZE,), ((0, 32),), -0.2, 0.2)), 0.2, 2.0)
    counts = draw_counts(jax.random.fold_in(arg_keys[7], 71), 0)
    return {"populations": populations, "solid": solid, "cell_index": cell_index, "offset": offset, "velocity": velocity, "mass": mass, "counts": counts}


LATTICE = np.array([[0, 0, 0], [1, 0, 0], [-1, 0, 0], [0, 1, 0], [0, -1, 0], [0, 0, 1], [0, 0, -1],
                    [1, 1, 0], [-1, -1, 0], [1, -1, 0], [-1, 1, 0], [1, 0, 1], [-1, 0, -1], [1, 0, -1], [-1, 0, 1],
                    [0, 1, 1], [0, -1, -1], [0, 1, -1], [0, -1, 1]])
WEIGHTS = [1.0 / 3.0] + [1.0 / 18.0] * 6 + [1.0 / 36.0] * 12
OPPOSITE = [int(np.where((LATTICE == -LATTICE[k]).all(1))[0][0]) for k in range(19)]
relax_time = 0.6
coupling = 0.5
settle = 0.02
body_force = 1e-4


def momenta(field):
    out = []
    for axis_id in range(3):
        total = jnp.zeros(field.shape[1:], jnp.float32)
        for index in range(19):
            if LATTICE[index, axis_id] != 0:
                total = total + float(LATTICE[index, axis_id]) * field[index]
        out.append(total)
    return out


def collide(field, force, solid):
    density = jnp.sum(field, axis=0)
    moment = momenta(field)
    flow = [(moment[d] + relax_time * force[d]) / density for d in range(3)]
    usq = flow[0] * flow[0] + flow[1] * flow[1] + flow[2] * flow[2]
    posts = []
    for index in range(19):
        along = jnp.zeros_like(density)
        for d in range(3):
            if LATTICE[index, d] != 0:
                along = along + float(LATTICE[index, d]) * flow[d]
        feq = WEIGHTS[index] * density * (1.0 + 3.0 * along + 4.5 * along * along - 1.5 * usq)
        posts.append(field[index] - (field[index] - feq) / relax_time)
    post = jnp.stack(posts)
    return jnp.where(solid[None] > 0, field[jnp.array(OPPOSITE)], post)


def reference(populations, solid, cell_index, offset, velocity, mass, counts):
    nx_all, ny_all, nz_all = populations.shape[1:]
    density = jnp.sum(populations, axis=0)
    cell_velocity = jnp.stack([m / density for m in momenta(populations)])
    slots = jnp.arange(PARTS_SIZE, dtype=jnp.int32)
    block = slots // P_CAP
    live = ((slots % P_CAP) < counts.reshape(-1)[block]).astype(jnp.float32)
    local_x = cell_index // (NY * CZ)
    ypos = (cell_index // CZ) % NY
    zpos = (block % N_GZ) * CZ + cell_index % CZ
    xpos = (block // N_GZ) * CX + local_x
    xnext = (xpos + 1) % nx_all
    here = cell_velocity[:, xpos, ypos, zpos]
    ahead = cell_velocity[:, xnext, ypos, zpos]
    particle_flow = (1.0 - offset) * here + offset * ahead
    change = coupling * live * (particle_flow - velocity)
    new_velocity = (velocity + change).at[1].add(-settle * live)
    push = -mass * change
    force = jnp.zeros((3, nx_all, ny_all, nz_all), jnp.float32)
    force = force.at[:, xpos, ypos, zpos].add(push * (1.0 - offset))
    force = force.at[:, xnext, ypos, zpos].add(push * offset)
    force = force.at[0].add(body_force)
    field = populations
    for step in range(SUBSTEPS):
        post = collide(field, force, solid)
        field = jnp.stack([jnp.roll(post[k], (int(LATTICE[k, 0]), int(LATTICE[k, 1]), int(LATTICE[k, 2])), axis=(0, 1, 2)) for k in range(19)])
    return field, new_velocity
```

```python
import functools

import jax
import jax.numpy as jnp
import numpy as np
from jax import lax
from jax.experimental import pallas as pl
from jax.experimental.pallas import tpu as pltpu
from jax.sharding import PartitionSpec as P

SUBSTEPS = 2

LATTICE = [
    (0, 0, 0),
    (1, 0, 0),
    (-1, 0, 0),
    (0, 1, 0),
    (0, -1, 0),
    (0, 0, 1),
    (0, 0, -1),
    (1, 1, 0),
    (-1, -1, 0),
    (1, -1, 0),
    (-1, 1, 0),
    (1, 0, 1),
    (-1, 0, -1),
    (1, 0, -1),
    (-1, 0, 1),
    (0, 1, 1),
    (0, -1, -1),
    (0, 1, -1),
    (0, -1, 1),
]
WEIGHTS = [1.0 / 3.0] + [1.0 / 18.0] * 6 + [1.0 / 36.0] * 12
relax_time = 0.6
coupling = 0.5
settle = 0.02
body_force = 0.0001

PAIRS = [(k, k + 1) for k in range(1, 19, 2)]
XP = [k for k in range(19) if LATTICE[k][0] == 1]
XM = [k for k in range(19) if LATTICE[k][0] == -1]
X0 = [k for k in range(19) if LATTICE[k][0] == 0]
ORDER = XP + XM + X0
PLACE = {k: i for i, k in enumerate(ORDER)}
ZP = [k for k in range(19) if LATTICE[k][2] == 1]
ZM = [k for k in range(19) if LATTICE[k][2] == -1]
LANES = {}
for _k in ZP + ZM:
    for _x in range(2):
        LANES[_k, _x] = len(LANES)


def halves(value):
    high = value.astype(jnp.bfloat16).astype(jnp.float32)
    return high, value - high


def total_of(terms):
    while len(terms) > 1:
        terms = [
            terms[i] + terms[i + 1] if i + 1 < len(terms) else terms[i]
            for i in range(0, len(terms), 2)
        ]
    return terms[0]


def moments(f):
    rho = total_of(list(f))
    mom = []
    for d in range(3):
        up = [f[k] for k in range(19) if LATTICE[k][d] == 1]
        down = [f[k] for k in range(19) if LATTICE[k][d] == -1]
        mom.append(total_of(up) - total_of(down))
    return rho, mom


def kernel(
    n_gx, n_gz,
    pops_in, solid_in, idx_in, off_in, vel_in, mass_in, counts_in,
    pops_out, vel_out,
    f_v, solid_v, idx_v, off_v, vel_v, mass_v, counts_v, nv_v, out_v, post_v,
    onehot_v, coef_v, vsend, vrecv, ssend, srecv, xp_recv, xm_recv, zsend, zrecv,
    in_sem, out_sem, vs_sem, vr_sem, ss_sem, sr_sem, x_ss, x_rs, z_ss, z_rs,
):
    gx, gz = lax.axis_index("gx"), lax.axis_index("gz")
    right, left = lax.rem(gx + 1, n_gx), lax.rem(gx + n_gx - 1, n_gx)
    xpos = {-1: left, 0: gx, 1: right}
    zdirs = (1,) if n_gz == 2 else (1, -1)
    zpos = {1: lax.rem(gz + 1, n_gz), -1: lax.rem(gz + n_gz - 1, n_gz), 0: gz}

    loads = [
        pltpu.make_async_copy(src, dst, in_sem.at[i])
        for i, (src, dst) in enumerate(
            [
                (pops_in, f_v),
                (idx_in, idx_v),
                (off_in, off_v),
                (mass_in, mass_v),
                (vel_in, vel_v),
                (counts_in, counts_v),
                (solid_in, solid_v),
            ]
        )
    ]
    for load in loads:
        load.start()

    peers = [(dx, dz) for dz in (0,) + zdirs for dx in (-1, 0, 1) if (dx, dz) != (0, 0)]
    barrier = pltpu.get_barrier_semaphore()
    for dx, dz in peers:
        pl.semaphore_signal(
            barrier,
            inc=1,
            device_id={"gx": xpos[dx], "gz": zpos[dz]},
            device_id_type=pl.DeviceIdType.MESH,
        )

    def send(src, dst, send_sem, recv_sem, dx, dz):
        copy = pltpu.make_async_remote_copy(
            src_ref=src,
            dst_ref=dst,
            send_sem=send_sem,
            recv_sem=recv_sem,
            device_id={"gx": xpos[dx], "gz": zpos[dz]},
            device_id_type=pl.DeviceIdType.MESH,
        )
        copy.start()
        return copy

    sent = []
    ny, nz = f_v.shape[2], f_v.shape[3]
    slots = idx_v.shape[0] * idx_v.shape[1]
    zbits, ybits = nz.bit_length() - 1, ny.bit_length() - 1

    for load in loads[1:6]:
        load.wait()

    def row(ref):
        return jnp.concatenate([ref[j : j + 1, :] for j in range(ref.shape[0])], axis=1)

    idx, off, mass = row(idx_v), row(off_v), row(mass_v)
    live = lax.broadcasted_iota(jnp.int32, (1, slots), 1) < counts_v[...]
    live = jnp.where(live, 1.0, 0.0).astype(jnp.float32)
    yidx = (idx >> zbits) & (ny - 1)
    key = ((idx >> (zbits + ybits)) << zbits) | (idx & (nz - 1))
    onehot_v[...] = jnp.where(
        lax.broadcasted_iota(jnp.int32, (2 * nz, slots), 0) == key, 1.0, 0.0
    ).astype(jnp.bfloat16)
    ymask = lax.broadcasted_iota(jnp.int32, (ny, slots), 0) == yidx
    near = 1.0 - off
    weight = (coupling * live) * mass
    wnear, wfar = weight * near, weight * off
    vel = [vel_v[d : d + 1, :] for d in range(3)]
    channels = [wnear * near, wnear * off, wfar * off]
    channels += [wnear * vel[d] for d in range(3)]
    channels += [wfar * vel[d] for d in range(3)]
    n_ch = len(channels)
    for c, channel in enumerate(channels):
        for h, part in enumerate(halves(channel)):
            at = (h * n_ch + c) * ny
            coef_v[at : at + ny, :] = jnp.where(ymask, part, 0.0).astype(jnp.bfloat16)

    loads[0].wait()
    f = [f_v[k] for k in range(19)]
    rho, mom = moments(f)
    inv = 1.0 / rho
    v = [m * inv for m in mom]
    for d in range(3):
        vsend[d] = v[d][0]
    pl.semaphore_wait(barrier, len(peers))
    v_copy = send(vsend, vrecv, vs_sem, vr_sem, -1, 0)
    sent.append(v_copy)

    sums = lax.dot_general(
        coef_v[...],
        onehot_v[...],
        (((1,), (1,)), ((), ())),
        preferred_element_type=jnp.float32,
    )
    sums = sums[: n_ch * ny] + sums[n_ch * ny :]

    def moment(c, x):
        return sums[c * ny : (c + 1) * ny, x * nz : (x + 1) * nz]

    a = [moment(0, x) for x in range(2)]
    b = [moment(1, x) for x in range(2)]
    e = [moment(2, x) for x in range(2)]
    q = [[moment(3 + d, x) for x in range(2)] for d in range(3)]
    r = [[moment(6 + d, x) for x in range(2)] for d in range(3)]
    for d in range(3):
        ssend[d] = r[d][1] - b[1] * v[d][1]
    ssend[3] = e[1]
    s_copy = send(ssend, srecv, ss_sem, sr_sem, 1, 0)
    sent.append(s_copy)

    loads[6].wait()
    solid = solid_v[...] > 0
    lane = lax.broadcasted_iota(jnp.int32, (ny, nz), 1)

    v_copy.wait_recv()
    s_copy.wait_recv()
    force = []
    for d in range(3):
        extra = body_force if d == 0 else 0.0
        first = q[d][0] - a[0] * v[d][0] - b[0] * v[d][1]
        first = first + (srecv[d] - srecv[3] * v[d][0]) + extra
        second = q[d][1] - a[1] * v[d][1] - b[1] * vrecv[d]
        second = second + (r[d][0] - b[0] * v[d][0] - e[0] * v[d][1]) + extra
        force.append(jnp.stack([first, second]) * relax_time)

    def particles():
        flows = []
        here = [jnp.concatenate([v[d][0], v[d][1]], axis=1) for d in range(3)]
        ahead = [jnp.concatenate([v[d][1], vrecv[d]], axis=1) for d in range(3)]
        table = jnp.concatenate(here + ahead, axis=0)
        high, low = halves(table)
        oh = onehot_v[...]
        found = jnp.dot(high.astype(jnp.bfloat16), oh, preferred_element_type=jnp.float32)
        found = found + jnp.dot(low.astype(jnp.bfloat16), oh, preferred_element_type=jnp.float32)
        for d in range(3):
            mix = near * found[d * ny : (d + 1) * ny] + off * found[(3 + d) * ny : (4 + d) * ny]
            flow = jnp.sum(jnp.where(ymask, mix, 0.0), axis=0, keepdims=True)
            new = vel[d] + coupling * live * (flow - vel[d])
            if d == 1:
                new = new - settle * live
            nv_v[d : d + 1, :] = new
        copy = pltpu.make_async_copy(nv_v, vel_out, out_sem.at[1])
        copy.start()
        return copy

    for step in range(SUBSTEPS):
        if step:
            rho, mom = moments(f)
            inv = 1.0 / rho
        post = post_v.at[step]
        u = [(mom[d] + force[d]) * inv for d in range(3)]
        usq = u[0] * u[0] + u[1] * u[1] + u[2] * u[2]
        scale = rho * (1.0 / relax_time)
        base = scale * (1.0 - 1.5 * usq)
        keep = 1.0 - 1.0 / relax_time
        by = {}

        def pair(k, o):
            w = WEIGHTS[k]
            along = total_of(
                [u[d] if LATTICE[k][d] == 1 else -u[d] for d in range(3) if LATTICE[k][d]]
            )
            lift = scale * along
            even = w * base + (4.5 * w) * (lift * along)
            odd = (3.0 * w) * lift
            by[k] = jnp.where(solid, f[o], keep * f[k] + (even + odd))
            by[o] = jnp.where(solid, f[k], keep * f[o] + (even - odd))
            post[PLACE[k]] = by[k]
            post[PLACE[o]] = by[o]

        for k, o in PAIRS:
            if LATTICE[k][0]:
                pair(k, o)
        xp_copy = send(
            post.at[0:5, 1], xp_recv.at[step], x_ss.at[step, 0], x_rs.at[step, 0], 1, 0
        )
        xm_copy = send(
            post.at[5:10, 0], xm_recv.at[step], x_ss.at[step, 1], x_rs.at[step, 1], -1, 0
        )
        for k, o in PAIRS:
            if not LATTICE[k][0] and LATTICE[k][2]:
                pair(k, o)
        packed = jnp.zeros((ny, nz), jnp.float32)
        for (k, x), at in LANES.items():
            edge = nz - 1 if LATTICE[k][2] == 1 else 0
            column = jnp.broadcast_to(by[k][x][:, edge : edge + 1], (ny, nz))
            packed = jnp.where(lane == at, column, packed)
        zsend[step] = packed
        z_copies = []
        for s, dz in enumerate(zdirs):
            for dx in (-1, 1, 0):
                z_copies.append(
                    send(
                        zsend.at[step],
                        zrecv.at[step, s, 1 - dx],
                        z_ss.at[step, s, 1 - dx],
                        z_rs.at[step, s, 1 - dx],
                        dx,
                        dz,
                    )
                )
        for k, o in PAIRS:
            if not LATTICE[k][0] and not LATTICE[k][2]:
                pair(k, o)
        by[0] = jnp.where(solid, f[0], keep * f[0] + WEIGHTS[0] * base)
        if step == 0:
            vel_copy = particles()
        xp_copy.wait_recv()
        xm_copy.wait_recv()
        for copy in z_copies:
            copy.wait_recv()
        sent += [xp_copy, xm_copy] + z_copies
        nf = []
        for k in range(19):
            cx, cy, cz = LATTICE[k]
            if cx == 1:
                planes = [(xp_recv[step, XP.index(k)], 0, 1), (by[k][0], 1, 0)]
            elif cx == -1:
                planes = [(by[k][1], 1, 1), (xm_recv[step, XM.index(k)], 2, 0)]
            else:
                planes = [(by[k][0], 1, 0), (by[k][1], 1, 1)]
            done = []
            for plane, source, x in planes:
                if cz:
                    s = 0 if cz == 1 else len(zdirs) - 1
                    at = LANES[k, x]
                    column = zrecv[step, s, source, :, at : at + 1]
                    plane = pltpu.roll(plane, 1 if cz == 1 else nz - 1, 1)
                    plane = jnp.where(
                        lane == (0 if cz == 1 else nz - 1),
                        jnp.broadcast_to(column, (ny, nz)),
                        plane,
                    )
                if cy:
                    plane = pltpu.roll(plane, 1 if cy == 1 else ny - 1, 0)
                done.append(plane)
            if step == SUBSTEPS - 1:
                out_v[k, 0] = done[0]
                out_v[k, 1] = done[1]
            else:
                nf.append(jnp.stack(done))
        f = nf

    out_copy = pltpu.make_async_copy(out_v, pops_out, out_sem.at[0])
    out_copy.start()
    for copy in sent:
        copy.wait_send()
    vel_copy.wait()
    out_copy.wait()


def body(n_gx, n_gz, populations, solid, cell_index, offset, velocity, mass, counts):
    depth_x, ny, nz = populations.shape[1:]
    slots = cell_index.shape[0]
    rows = (slots // nz, nz)
    nzs = 1 if n_gz == 2 else 2
    f32, vmem, dma = jnp.float32, pltpu.VMEM, pltpu.SemaphoreType.DMA
    return pl.pallas_call(
        functools.partial(kernel, n_gx, n_gz),
        out_shape=(
            jax.ShapeDtypeStruct(populations.shape, f32),
            jax.ShapeDtypeStruct(velocity.shape, f32),
        ),
        in_specs=[pl.BlockSpec(memory_space=pl.ANY)] * 7,
        out_specs=[pl.BlockSpec(memory_space=pl.ANY)] * 2,
        scratch_shapes=[
            vmem(populations.shape, f32),
            vmem(solid.shape, jnp.int32),
            vmem(rows, jnp.int32),
            vmem(rows, f32),
            vmem(velocity.shape, f32),
            vmem(rows, f32),
            vmem((1, 1), jnp.int32),
            vmem(velocity.shape, f32),
            vmem(populations.shape, f32),
            vmem((SUBSTEPS,) + populations.shape, f32),
            vmem((2 * nz, slots), jnp.bfloat16),
            vmem((18 * ny, slots), jnp.bfloat16),
            vmem((3, ny, nz), f32),
            vmem((3, ny, nz), f32),
            vmem((4, ny, nz), f32),
            vmem((4, ny, nz), f32),
            vmem((SUBSTEPS, 5, ny, nz), f32),
            vmem((SUBSTEPS, 5, ny, nz), f32),
            vmem((SUBSTEPS, ny, nz), f32),
            vmem((SUBSTEPS, nzs, 3, ny, nz), f32),
            dma((7,)),
            dma((2,)),
            dma,
            dma,
            dma,
            dma,
            dma((SUBSTEPS, 2)),
            dma((SUBSTEPS, 2)),
            dma((SUBSTEPS, nzs, 3)),
            dma((SUBSTEPS, nzs, 3)),
        ],
        compiler_params=pltpu.CompilerParams(
            collective_id=0, has_side_effects=True, vmem_limit_bytes=32 * 1024 * 1024
        ),
    )(
        populations,
        solid,
        cell_index.reshape(rows),
        offset.reshape(rows),
        velocity,
        mass.reshape(rows),
        counts,
    )


def solution(mesh):
    return jax.shard_map(
        functools.partial(body, mesh.shape["gx"], mesh.shape["gz"]),
        mesh=mesh,
        in_specs=(
            P(None, "gx", None, "gz"),
            P("gx", None, "gz"),
            P(("gx", "gz")),
            P(("gx", "gz")),
            P(None, ("gx", "gz")),
            P(("gx", "gz")),
            P("gx", "gz"),
        ),
        out_specs=(P(None, "gx", None, "gz"), P(None, ("gx", "gz"))),
        check_vma=False,
    )
```

```python
import functools

import jax
import jax.numpy as jnp
import numpy as np
from jax import lax
from jax.experimental import pallas as pl
from jax.experimental.pallas import tpu as pltpu
from jax.sharding import PartitionSpec as P

SUBSTEPS = 2

LATTICE = [
    (0, 0, 0),
    (1, 0, 0),
    (-1, 0, 0),
    (0, 1, 0),
    (0, -1, 0),
    (0, 0, 1),
    (0, 0, -1),
    (1, 1, 0),
    (-1, -1, 0),
    (1, -1, 0),
    (-1, 1, 0),
    (1, 0, 1),
    (-1, 0, -1),
    (1, 0, -1),
    (-1, 0, 1),
    (0, 1, 1),
    (0, -1, -1),
    (0, 1, -1),
    (0, -1, 1),
]
WEIGHTS = [1.0 / 3.0] + [1.0 / 18.0] * 6 + [1.0 / 36.0] * 12
relax_time = 0.6
coupling = 0.5
settle = 0.02
body_force = 0.0001

PAIRS = [(k, k + 1) for k in range(1, 19, 2)]
XP = [k for k in range(19) if LATTICE[k][0] == 1]
XM = [k for k in range(19) if LATTICE[k][0] == -1]
X0 = [k for k in range(19) if LATTICE[k][0] == 0]
ORDER = XP + XM + X0
PLACE = {k: i for i, k in enumerate(ORDER)}
ZP = [k for k in range(19) if LATTICE[k][2] == 1]
ZM = [k for k in range(19) if LATTICE[k][2] == -1]
LANES = {}
for _k in ZP + ZM:
    for _x in range(2):
        LANES[_k, _x] = len(LANES)


def halves(value):
    high = value.astype(jnp.bfloat16).astype(jnp.float32)
    return high, value - high


def total_of(terms):
    while len(terms) > 1:
        terms = [
            terms[i] + terms[i + 1] if i + 1 < len(terms) else terms[i]
            for i in range(0, len(terms), 2)
        ]
    return terms[0]


def moments(f):
    rho = total_of(list(f))
    mom = []
    for d in range(3):
        up = [f[k] for k in range(19) if LATTICE[k][d] == 1]
        down = [f[k] for k in range(19) if LATTICE[k][d] == -1]
        mom.append(total_of(up) - total_of(down))
    return rho, mom


def kernel(
    n_gx, n_gz,
    pops_in, solid_in, idx_in, off_in, vel_in, mass_in, counts_in,
    out_v, nv_v,
    f_v, solid_v, idx_v, off_v, vel_v, mass_v, counts_v, post_v,
    onehot_v, coef_v, vsend, vrecv, ssend, srecv, xp_recv, xm_recv, zsend, zrecv,
    in_sem, vs_sem, vr_sem, ss_sem, sr_sem, x_ss, x_rs, z_ss, z_rs,
):
    gx, gz = lax.axis_index("gx"), lax.axis_index("gz")
    right, left = lax.rem(gx + 1, n_gx), lax.rem(gx + n_gx - 1, n_gx)
    xpos = {-1: left, 0: gx, 1: right}
    zdirs = (1,) if n_gz == 2 else (1, -1)
    zpos = {1: lax.rem(gz + 1, n_gz), -1: lax.rem(gz + n_gz - 1, n_gz), 0: gz}

    loads = [
        pltpu.make_async_copy(src, dst, in_sem.at[i])
        for i, (src, dst) in enumerate(
            [
                (pops_in, f_v),
                (idx_in, idx_v),
                (off_in, off_v),
                (mass_in, mass_v),
                (vel_in, vel_v),
                (counts_in, counts_v),
                (solid_in, solid_v),
            ]
        )
    ]
    for load in loads:
        load.start()

    peers = [(dx, dz) for dz in (0,) + zdirs for dx in (-1, 0, 1) if (dx, dz) != (0, 0)]
    barrier = pltpu.get_barrier_semaphore()
    for dx, dz in peers:
        pl.semaphore_signal(
            barrier,
            inc=1,
            device_id={"gx": xpos[dx], "gz": zpos[dz]},
            device_id_type=pl.DeviceIdType.MESH,
        )

    def send(src, dst, send_sem, recv_sem, dx, dz):
        copy = pltpu.make_async_remote_copy(
            src_ref=src,
            dst_ref=dst,
            send_sem=send_sem,
            recv_sem=recv_sem,
            device_id={"gx": xpos[dx], "gz": zpos[dz]},
            device_id_type=pl.DeviceIdType.MESH,
        )
        copy.start()
        return copy

    sent = []
    ny, nz = f_v.shape[2], f_v.shape[3]
    slots = idx_v.shape[0] * idx_v.shape[1]
    zbits, ybits = nz.bit_length() - 1, ny.bit_length() - 1

    for load in loads[1:6]:
        load.wait()

    def row(ref):
        return jnp.concatenate([ref[j : j + 1, :] for j in range(ref.shape[0])], axis=1)

    idx, off, mass = row(idx_v), row(off_v), row(mass_v)
    live = lax.broadcasted_iota(jnp.int32, (1, slots), 1) < counts_v[...]
    live = jnp.where(live, 1.0, 0.0).astype(jnp.float32)
    yidx = (idx >> zbits) & (ny - 1)
    key = ((idx >> (zbits + ybits)) << zbits) | (idx & (nz - 1))
    onehot_v[...] = jnp.where(
        lax.broadcasted_iota(jnp.int32, (2 * nz, slots), 0) == key, 1.0, 0.0
    ).astype(jnp.bfloat16)
    ymask = lax.broadcasted_iota(jnp.int32, (ny, slots), 0) == yidx
    near = 1.0 - off
    weight = (coupling * live) * mass
    wnear, wfar = weight * near, weight * off
    vel = [vel_v[d : d + 1, :] for d in range(3)]
    channels = [wnear * near, wnear * off, wfar * off]
    channels += [wnear * vel[d] for d in range(3)]
    channels += [wfar * vel[d] for d in range(3)]
    n_ch = len(channels)
    for c, channel in enumerate(channels):
        for h, part in enumerate(halves(channel)):
            at = (h * n_ch + c) * ny
            coef_v[at : at + ny, :] = jnp.where(ymask, part, 0.0).astype(jnp.bfloat16)

    loads[0].wait()
    f = [f_v[k] for k in range(19)]
    rho, mom = moments(f)
    inv = 1.0 / rho
    v = [m * inv for m in mom]
    for d in range(3):
        vsend[d] = v[d][0]
    pl.semaphore_wait(barrier, len(peers))
    v_copy = send(vsend, vrecv, vs_sem, vr_sem, -1, 0)
    sent.append(v_copy)

    sums = lax.dot_general(
        coef_v[...],
        onehot_v[...],
        (((1,), (1,)), ((), ())),
        preferred_element_type=jnp.float32,
    )
    sums = sums[: n_ch * ny] + sums[n_ch * ny :]

    def moment(c, x):
        return sums[c * ny : (c + 1) * ny, x * nz : (x + 1) * nz]

    a = [moment(0, x) for x in range(2)]
    b = [moment(1, x) for x in range(2)]
    e = [moment(2, x) for x in range(2)]
    q = [[moment(3 + d, x) for x in range(2)] for d in range(3)]
    r = [[moment(6 + d, x) for x in range(2)] for d in range(3)]
    for d in range(3):
        ssend[d] = r[d][1] - b[1] * v[d][1]
    ssend[3] = e[1]
    s_copy = send(ssend, srecv, ss_sem, sr_sem, 1, 0)
    sent.append(s_copy)

    loads[6].wait()
    solid = solid_v[...] > 0
    lane = lax.broadcasted_iota(jnp.int32, (ny, nz), 1)

    v_copy.wait_recv()
    s_copy.wait_recv()
    force = []
    for d in range(3):
        extra = body_force if d == 0 else 0.0
        first = q[d][0] - a[0] * v[d][0] - b[0] * v[d][1]
        first = first + (srecv[d] - srecv[3] * v[d][0]) + extra
        second = q[d][1] - a[1] * v[d][1] - b[1] * vrecv[d]
        second = second + (r[d][0] - b[0] * v[d][0] - e[0] * v[d][1]) + extra
        force.append(jnp.stack([first, second]) * relax_time)

    def particles():
        flows = []
        here = [jnp.concatenate([v[d][0], v[d][1]], axis=1) for d in range(3)]
        ahead = [jnp.concatenate([v[d][1], vrecv[d]], axis=1) for d in range(3)]
        table = jnp.concatenate(here + ahead, axis=0)
        high, low = halves(table)
        oh = onehot_v[...]
        found = jnp.dot(high.astype(jnp.bfloat16), oh, preferred_element_type=jnp.float32)
        found = found + jnp.dot(low.astype(jnp.bfloat16), oh, preferred_element_type=jnp.float32)
        for d in range(3):
            mix = near * found[d * ny : (d + 1) * ny] + off * found[(3 + d) * ny : (4 + d) * ny]
            flow = jnp.sum(jnp.where(ymask, mix, 0.0), axis=0, keepdims=True)
            new = vel[d] + coupling * live * (flow - vel[d])
            if d == 1:
                new = new - settle * live
            nv_v[d : d + 1, :] = new

    for step in range(SUBSTEPS):
        if step:
            rho, mom = moments(f)
            inv = 1.0 / rho
        post = post_v.at[step]
        u = [(mom[d] + force[d]) * inv for d in range(3)]
        usq = u[0] * u[0] + u[1] * u[1] + u[2] * u[2]
        scale = rho * (1.0 / relax_time)
        base = scale * (1.0 - 1.5 * usq)
        keep = 1.0 - 1.0 / relax_time
        by = {}

        def pair(k, o):
            w = WEIGHTS[k]
            along = total_of(
                [u[d] if LATTICE[k][d] == 1 else -u[d] for d in range(3) if LATTICE[k][d]]
            )
            lift = scale * along
            even = w * base + (4.5 * w) * (lift * along)
            odd = (3.0 * w) * lift
            by[k] = jnp.where(solid, f[o], keep * f[k] + (even + odd))
            by[o] = jnp.where(solid, f[k], keep * f[o] + (even - odd))
            post[PLACE[k]] = by[k]
            post[PLACE[o]] = by[o]

        for k, o in PAIRS:
            if LATTICE[k][0]:
                pair(k, o)
        xp_copy = send(
            post.at[0:5, 1], xp_recv.at[step], x_ss.at[step, 0], x_rs.at[step, 0], 1, 0
        )
        xm_copy = send(
            post.at[5:10, 0], xm_recv.at[step], x_ss.at[step, 1], x_rs.at[step, 1], -1, 0
        )
        for k, o in PAIRS:
            if not LATTICE[k][0] and LATTICE[k][2]:
                pair(k, o)
        packed = jnp.zeros((ny, nz), jnp.float32)
        for (k, x), at in LANES.items():
            edge = nz - 1 if LATTICE[k][2] == 1 else 0
            column = jnp.broadcast_to(by[k][x][:, edge : edge + 1], (ny, nz))
            packed = jnp.where(lane == at, column, packed)
        zsend[step] = packed
        z_copies = []
        for s, dz in enumerate(zdirs):
            for dx in (-1, 1, 0):
                z_copies.append(
                    send(
                        zsend.at[step],
                        zrecv.at[step, s, 1 - dx],
                        z_ss.at[step, s, 1 - dx],
                        z_rs.at[step, s, 1 - dx],
                        dx,
                        dz,
                    )
                )
        for k, o in PAIRS:
            if not LATTICE[k][0] and not LATTICE[k][2]:
                pair(k, o)
        by[0] = jnp.where(solid, f[0], keep * f[0] + WEIGHTS[0] * base)
        if step == 0:
            particles()
        xp_copy.wait_recv()
        xm_copy.wait_recv()
        for copy in z_copies:
            copy.wait_recv()
        sent += [xp_copy, xm_copy] + z_copies
        nf = []
        for k in range(19):
            cx, cy, cz = LATTICE[k]
            if cx == 1:
                planes = [(xp_recv[step, XP.index(k)], 0, 1), (by[k][0], 1, 0)]
            elif cx == -1:
                planes = [(by[k][1], 1, 1), (xm_recv[step, XM.index(k)], 2, 0)]
            else:
                planes = [(by[k][0], 1, 0), (by[k][1], 1, 1)]
            done = []
            for plane, source, x in planes:
                if cz:
                    s = 0 if cz == 1 else len(zdirs) - 1
                    at = LANES[k, x]
                    column = zrecv[step, s, source, :, at : at + 1]
                    plane = pltpu.roll(plane, 1 if cz == 1 else nz - 1, 1)
                    plane = jnp.where(
                        lane == (0 if cz == 1 else nz - 1),
                        jnp.broadcast_to(column, (ny, nz)),
                        plane,
                    )
                if cy:
                    plane = pltpu.roll(plane, 1 if cy == 1 else ny - 1, 0)
                done.append(plane)
            if step == SUBSTEPS - 1:
                out_v[k, 0] = done[0]
                out_v[k, 1] = done[1]
            else:
                nf.append(jnp.stack(done))
        f = nf

    for copy in sent:
        copy.wait_send()


def store(a_in, b_in, a_out, b_out, sems):
    copies = [
        pltpu.make_async_copy(a_in, a_out, sems.at[0]),
        pltpu.make_async_copy(b_in, b_out, sems.at[1]),
    ]
    for copy in copies:
        copy.start()
    for copy in copies:
        copy.wait()


def body(n_gx, n_gz, populations, solid, cell_index, offset, velocity, mass, counts):
    depth_x, ny, nz = populations.shape[1:]
    slots = cell_index.shape[0]
    rows = (slots // nz, nz)
    nzs = 1 if n_gz == 2 else 2
    f32, vmem, dma = jnp.float32, pltpu.VMEM, pltpu.SemaphoreType.DMA
    shapes = (
        jax.ShapeDtypeStruct(populations.shape, f32),
        jax.ShapeDtypeStruct(velocity.shape, f32),
    )
    held = pl.pallas_call(
        functools.partial(kernel, n_gx, n_gz),
        out_shape=shapes,
        in_specs=[pl.BlockSpec(memory_space=pltpu.HBM)] * 6
        + [pl.BlockSpec(memory_space=pl.ANY)],
        out_specs=[pl.BlockSpec(memory_space=pltpu.VMEM)] * 2,
        scratch_shapes=[
            vmem(populations.shape, f32),
            vmem(solid.shape, jnp.int32),
            vmem(rows, jnp.int32),
            vmem(rows, f32),
            vmem(velocity.shape, f32),
            vmem(rows, f32),
            vmem((1, 1), jnp.int32),
            vmem((SUBSTEPS,) + populations.shape, f32),
            vmem((2 * nz, slots), jnp.bfloat16),
            vmem((18 * ny, slots), jnp.bfloat16),
            vmem((3, ny, nz), f32),
            vmem((3, ny, nz), f32),
            vmem((4, ny, nz), f32),
            vmem((4, ny, nz), f32),
            vmem((SUBSTEPS, 5, ny, nz), f32),
            vmem((SUBSTEPS, 5, ny, nz), f32),
            vmem((SUBSTEPS, ny, nz), f32),
            vmem((SUBSTEPS, nzs, 3, ny, nz), f32),
            dma((7,)),
            dma,
            dma,
            dma,
            dma,
            dma((SUBSTEPS, 2)),
            dma((SUBSTEPS, 2)),
            dma((SUBSTEPS, nzs, 3)),
            dma((SUBSTEPS, nzs, 3)),
        ],
        compiler_params=pltpu.CompilerParams(
            collective_id=0, has_side_effects=True, vmem_limit_bytes=32 * 1024 * 1024
        ),
    )(
        *[
            pltpu.with_memory_space_constraint(value, pltpu.HBM)
            for value in (
                populations,
                solid,
                cell_index.reshape(rows),
                offset.reshape(rows),
                velocity,
                mass.reshape(rows),
            )
        ],
        counts,
    )
    return pl.pallas_call(
        store,
        out_shape=shapes,
        in_specs=[pl.BlockSpec(memory_space=pltpu.VMEM)] * 2,
        out_specs=[pl.BlockSpec(memory_space=pltpu.HBM)] * 2,
        scratch_shapes=[dma((2,))],
        compiler_params=pltpu.CompilerParams(vmem_limit_bytes=2 * 1024 * 1024),
    )(*held)


def solution(mesh):
    return jax.shard_map(
        functools.partial(body, mesh.shape["gx"], mesh.shape["gz"]),
        mesh=mesh,
        in_specs=(
            P(None, "gx", None, "gz"),
            P("gx", None, "gz"),
            P(("gx", "gz")),
            P(("gx", "gz")),
            P(None, ("gx", "gz")),
            P(("gx", "gz")),
            P("gx", "gz"),
        ),
        out_specs=(P(None, "gx", None, "gz"), P(None, ("gx", "gz"))),
        check_vma=False,
    )
```

```python
import functools

import jax
import jax.numpy as jnp
from jax import lax
from jax.experimental import pallas as pl
from jax.experimental.pallas import tpu as pltpu
from jax.sharding import PartitionSpec as P

LATTICE = [
    (0, 0, 0),
    (1, 0, 0),
    (-1, 0, 0),
    (0, 1, 0),
    (0, -1, 0),
    (0, 0, 1),
    (0, 0, -1),
    (1, 1, 0),
    (-1, -1, 0),
    (1, -1, 0),
    (-1, 1, 0),
    (1, 0, 1),
    (-1, 0, -1),
    (1, 0, -1),
    (-1, 0, 1),
    (0, 1, 1),
    (0, -1, -1),
    (0, 1, -1),
    (0, -1, 1),
]
WEIGHTS = [1.0 / 3.0] + [1.0 / 18.0] * 6 + [1.0 / 36.0] * 12
relax_time = 0.6
coupling = 0.5
settle = 0.02
body_force = 0.0001

OPPOSITE = [0] + [k + 1 if k % 2 else k - 1 for k in range(1, 19)]
XP = [k for k in range(19) if LATTICE[k][0] == 1]
XM = [k for k in range(19) if LATTICE[k][0] == -1]
ZP = [k for k in range(19) if LATTICE[k][2] == 1]
ZM = [k for k in range(19) if LATTICE[k][2] == -1]
LANES = {}
for _k in ZP + ZM:
    for _x in range(2):
        LANES[_k, _x] = len(LANES)


def halves(value):
    high = value.astype(jnp.bfloat16).astype(jnp.float32)
    return high, value - high


def total_of(terms):
    while len(terms) > 1:
        terms = [
            terms[i] + terms[i + 1] if i + 1 < len(terms) else terms[i]
            for i in range(0, len(terms), 2)
        ]
    return terms[0]


def moments(f):
    rho = total_of(list(f))
    mom = []
    for d in range(3):
        up = [f[k] for k in range(19) if LATTICE[k][d] == 1]
        down = [f[k] for k in range(19) if LATTICE[k][d] == -1]
        mom.append(total_of(up) - total_of(down))
    return rho, mom


def pair_terms(k, u, scale, base):
    w = WEIGHTS[k]
    along = total_of(
        [u[d] if LATTICE[k][d] == 1 else -u[d] for d in range(3) if LATTICE[k][d]]
    )
    lift = scale * along
    return w * base + (4.5 * w) * (lift * along), (3.0 * w) * lift


def collide(ks, kept, m, inv, scale):
    u = [value * inv for value in m]
    base = scale * (1.0 - 1.5 * (u[0] * u[0] + u[1] * u[1] + u[2] * u[2]))
    out, terms = {}, {}
    for k in ks:
        if k == 0:
            out[0] = kept[0] + WEIGHTS[0] * base
            continue
        first = k if k % 2 else k - 1
        if first not in terms:
            terms[first] = pair_terms(first, u, scale, base)
        even, odd = terms[first]
        out[k] = kept[k] + (even + odd if k == first else even - odd)
    return out


def kernel(
    n_gx, n_gz,
    pops_in, solid_in, idx_in, off_in, vel_in, mass_in, counts_in,
    out_v, nv_v,
    f_v, solid_v, idx_v, off_v, vel_v, mass_v, counts_v,
    onehot_v, coef_v, a1s, a1r, a2s, a2r, b1s, b1r, b2s, b2r,
    xp_send, xm_send, xp_recv, xm_recv, zsend, zrecv,
    in_sem, r_ss, r_rs, x_ss, x_rs, z_ss, z_rs,
):
    gx, gz = lax.axis_index("gx"), lax.axis_index("gz")
    right, left = lax.rem(gx + 1, n_gx), lax.rem(gx + n_gx - 1, n_gx)
    xpos = {-1: left, 0: gx, 1: right}
    zdirs = (1,) if n_gz == 2 else (1, -1)
    zpos = {1: lax.rem(gz + 1, n_gz), -1: lax.rem(gz + n_gz - 1, n_gz), 0: gz}

    loads = [
        pltpu.make_async_copy(src, dst, in_sem.at[i])
        for i, (src, dst) in enumerate(
            [
                (pops_in, f_v),
                (solid_in, solid_v),
                (idx_in, idx_v),
                (off_in, off_v),
                (mass_in, mass_v),
                (vel_in, vel_v),
                (counts_in, counts_v),
            ]
        )
    ]
    for load in loads:
        load.start()

    peers = [(dx, dz) for dz in (0,) + zdirs for dx in (-1, 0, 1) if (dx, dz) != (0, 0)]
    barrier = pltpu.get_barrier_semaphore()
    for dx, dz in peers:
        pl.semaphore_signal(
            barrier,
            inc=1,
            device_id={"gx": xpos[dx], "gz": zpos[dz]},
            device_id_type=pl.DeviceIdType.MESH,
        )

    sent = []

    def send(src, dst, send_sem, recv_sem, dx, dz):
        copy = pltpu.make_async_remote_copy(
            src_ref=src,
            dst_ref=dst,
            send_sem=send_sem,
            recv_sem=recv_sem,
            device_id={"gx": xpos[dx], "gz": zpos[dz]},
            device_id_type=pl.DeviceIdType.MESH,
        )
        copy.start()
        sent.append(copy)
        return copy

    def send_rim(step):
        return [
            send(
                zsend.at[step],
                zrecv.at[step, s, 1 - dx],
                z_ss.at[step, s, 1 - dx],
                z_rs.at[step, s, 1 - dx],
                dx,
                dz,
            )
            for s, dz in enumerate(zdirs)
            for dx in (-1, 1, 0)
        ]

    ny, nz = f_v.shape[2], f_v.shape[3]
    slots = idx_v.shape[0] * idx_v.shape[1]
    zbits, ybits = nz.bit_length() - 1, ny.bit_length() - 1
    lane = lax.broadcasted_iota(jnp.int32, (ny, nz), 1)
    keep = 1.0 - 1.0 / relax_time
    everything = list(range(19))

    def wide(column):
        return jnp.broadcast_to(column, (ny, nz))

    def pack(columns):
        packed = jnp.zeros((ny, nz), jnp.float32)
        for at, (tile, edge) in enumerate(columns):
            z = nz - 1 if edge == 0 else 0
            packed = jnp.where(lane == at, wide(tile[:, z : z + 1]), packed)
        return packed

    def rim(step, edge, source, at):
        s = 0 if edge == 0 else len(zdirs) - 1
        return wide(zrecv[step, s, source, :, at : at + 1])

    loads[0].wait()
    loads[1].wait()
    f = [f_v[k] for k in range(19)]
    solid = solid_v[...] > 0

    def cells(f):
        rho, mom = moments(f)
        scale = jnp.where(solid, 0.0, rho * (1.0 / relax_time))
        kept = [jnp.where(solid, f[OPPOSITE[k]], keep * f[k]) for k in range(19)]
        return mom, 1.0 / rho, scale, kept

    mom, inv, scale, kept = cells(f)
    v = [m * inv for m in mom]
    a1s[0] = scale[1]
    for i, k in enumerate(XP):
        a1s[1 + i] = kept[k][1]
    for d in range(3):
        b1s[d] = v[d][0]
    b1s[3] = scale[0]
    for i, k in enumerate(XM):
        b1s[4 + i] = kept[k][0]
    pl.semaphore_wait(barrier, len(peers))
    first = [
        send(b1s, b1r, r_ss.at[0], r_rs.at[0], -1, 0),
        send(a1s, a1r, r_ss.at[1], r_rs.at[1], 1, 0),
    ]

    for load in loads[2:]:
        load.wait()

    def row(ref):
        return jnp.concatenate([ref[j : j + 1, :] for j in range(ref.shape[0])], axis=1)

    idx, off, mass = row(idx_v), row(off_v), row(mass_v)
    live = lax.broadcasted_iota(jnp.int32, (1, slots), 1) < counts_v[...]
    live = jnp.where(live, 1.0, 0.0).astype(jnp.float32)
    yidx = (idx >> zbits) & (ny - 1)
    key = ((idx >> (zbits + ybits)) << zbits) | (idx & (nz - 1))
    onehot_v[...] = jnp.where(
        lax.broadcasted_iota(jnp.int32, (2 * nz, slots), 0) == key, 1.0, 0.0
    ).astype(jnp.bfloat16)
    ymask = lax.broadcasted_iota(jnp.int32, (ny, slots), 0) == yidx
    near = 1.0 - off
    weight = (coupling * live) * mass
    wnear, wfar = weight * near, weight * off
    vel = [vel_v[d : d + 1, :] for d in range(3)]
    channels = [wnear * near, wnear * off, wfar * off]
    channels += [wnear * vel[d] for d in range(3)]
    channels += [wfar * vel[d] for d in range(3)]
    n_ch = len(channels)
    for c, channel in enumerate(channels):
        for h, part in enumerate(halves(channel)):
            at = (h * n_ch + c) * ny
            coef_v[at : at + ny, :] = jnp.where(ymask, part, 0.0).astype(jnp.bfloat16)
    sums = lax.dot_general(
        coef_v[...],
        onehot_v[...],
        (((1,), (1,)), ((), ())),
        preferred_element_type=jnp.float32,
    )
    sums = (sums[: n_ch * ny] + sums[n_ch * ny :]) * relax_time

    def moment(c, x):
        return sums[c * ny : (c + 1) * ny, x * nz : (x + 1) * nz]

    a, b, e = [[moment(c, x) for x in range(2)] for c in range(3)]
    part0, part1, spill = [], [], []
    for d in range(3):
        q = [moment(3 + d, x) for x in range(2)]
        r = [moment(6 + d, x) for x in range(2)]
        extra = relax_time * body_force if d == 0 else 0.0
        part0.append(q[0] - a[0] * v[d][0] - b[0] * v[d][1] + extra)
        part1.append(
            (q[1] - a[1] * v[d][1]) + (r[0] - b[0] * v[d][0] - e[0] * v[d][1]) + extra
        )
        spill.append(r[1] - b[1] * v[d][1])
    m0 = [mom[d][0] + part0[d] for d in range(3)]
    m1 = [mom[d][1] + part1[d] for d in range(3)]
    for d in range(3):
        b2s[d] = m0[d]
        a2s[d] = spill[d]
        a2s[4 + d] = m1[d]
    a2s[3] = e[1]
    a2s[7] = b[1]
    first += [
        send(a2s, a2r, r_ss.at[2], r_rs.at[2], 1, 0),
        send(b2s, b2r, r_ss.at[3], r_rs.at[3], -1, 0),
    ]
    at0, at1, columns = {}, {}, []
    for edge, ks in enumerate((ZP, ZM)):
        at0[edge] = len(columns)
        for tile in [v[d][0] for d in range(3)] + m0 + [scale[0]] + [kept[k][0] for k in ks]:
            columns.append((tile, edge))
        at1[edge] = len(columns)
        for tile in spill + [e[1]] + m1 + [b[1], scale[1]] + [kept[k][1] for k in ks]:
            columns.append((tile, edge))
    zsend[0] = pack(columns)
    first += send_rim(0)

    for copy in first:
        copy.wait_recv()
    vfront = [b1r[d] for d in range(3)]
    force = [
        jnp.stack(
            [part0[d] + (a2r[d] - a2r[3] * v[d][0]), part1[d] - b[1] * vfront[d]]
        )
        for d in range(3)
    ]

    def inverse(scale):
        return 1.0 / (relax_time * jnp.where(scale > 0.0, scale, 1.0))

    by = collide(everything, kept, [mom[d] + force[d] for d in range(3)], inv, scale)
    before = collide(
        XP,
        {k: a1r[1 + i] for i, k in enumerate(XP)},
        [a2r[4 + d] - a2r[7] * v[d][0] for d in range(3)],
        inverse(a1r[0]),
        a1r[0],
    )
    after = collide(
        XM,
        {k: b1r[4 + i] for i, k in enumerate(XM)},
        [b2r[d] + (spill[d] - e[1] * vfront[d]) for d in range(3)],
        inverse(b1r[3]),
        b1r[3],
    )
    rims = {}
    for edge, ks in enumerate((ZP, ZM)):
        flow = {s: [rim(0, edge, s, at0[edge] + d) for d in range(3)] for s in (1, 2)}
        drag = {s: [rim(0, edge, s, at1[edge] + d) for d in range(4)] for s in (0, 1)}
        for source, x in ((1, 0), (1, 1), (0, 1), (2, 0)):
            want = [k for k in ks if source == 1 or LATTICE[k][0] == 1 - source]
            if x == 0:
                at = at0[edge] + 3
                t = drag[source - 1]
                m = [
                    rim(0, edge, source, at + d) + (t[d] - t[3] * flow[source][d])
                    for d in range(3)
                ]
                at = at + 3
            else:
                at = at1[edge] + 4
                ahead = rim(0, edge, source, at + 3)
                m = [
                    rim(0, edge, source, at + d) - ahead * flow[source + 1][d]
                    for d in range(3)
                ]
                at = at + 4
            cell_scale = rim(0, edge, source, at)
            known = {k: rim(0, edge, source, at + 1 + ks.index(k)) for k in want}
            post = collide(want, known, m, inverse(cell_scale), cell_scale)
            for k in want:
                rims[k, source, x] = post[k]

    def stream(k, by, before, after, column):
        cx, cy, cz = LATTICE[k]
        if cx == 1:
            planes = [(before[k], 0, 1), (by[k][0], 1, 0)]
        elif cx == -1:
            planes = [(by[k][1], 1, 1), (after[k], 2, 0)]
        else:
            planes = [(by[k][0], 1, 0), (by[k][1], 1, 1)]
        done = []
        for plane, source, x in planes:
            if cz:
                plane = pltpu.roll(plane, 1 if cz == 1 else nz - 1, 1)
                plane = jnp.where(
                    lane == (0 if cz == 1 else nz - 1), column(k, source, x), plane
                )
            if cy:
                plane = pltpu.roll(plane, 1 if cy == 1 else ny - 1, 0)
            done.append(plane)
        return done

    f = [
        jnp.stack(stream(k, by, before, after, lambda *key: rims[key])) for k in everything
    ]

    mom, inv, scale, kept = cells(f)
    by = collide(everything, kept, [mom[d] + force[d] for d in range(3)], inv, scale)
    for i, k in enumerate(XP):
        xp_send[i] = by[k][1]
    for i, k in enumerate(XM):
        xm_send[i] = by[k][0]
    last = [
        send(xp_send, xp_recv, x_ss.at[0], x_rs.at[0], 1, 0),
        send(xm_send, xm_recv, x_ss.at[1], x_rs.at[1], -1, 0),
    ]
    zsend[1] = pack([(by[k][x], 0 if LATTICE[k][2] == 1 else 1) for k, x in LANES])
    last += send_rim(1)

    here = [jnp.concatenate([v[d][0], v[d][1]], axis=1) for d in range(3)]
    ahead = [jnp.concatenate([v[d][1], vfront[d]], axis=1) for d in range(3)]
    high, low = halves(jnp.concatenate(here + ahead, axis=0))
    oh = onehot_v[...]
    found = jnp.dot(high.astype(jnp.bfloat16), oh, preferred_element_type=jnp.float32)
    found = found + jnp.dot(low.astype(jnp.bfloat16), oh, preferred_element_type=jnp.float32)
    for d in range(3):
        mix = near * found[d * ny : (d + 1) * ny] + off * found[(3 + d) * ny : (4 + d) * ny]
        flow = jnp.sum(jnp.where(ymask, mix, 0.0), axis=0, keepdims=True)
        new = vel[d] + coupling * live * (flow - vel[d])
        if d == 1:
            new = new - settle * live
        nv_v[d : d + 1, :] = new

    def column(k, source, x):
        return rim(1, 0 if LATTICE[k][2] == 1 else 1, source, LANES[k, x])

    for copy in last:
        copy.wait_recv()
    before = {k: xp_recv[i] for i, k in enumerate(XP)}
    after = {k: xm_recv[i] for i, k in enumerate(XM)}
    for k in everything:
        for x, plane in enumerate(stream(k, by, before, after, column)):
            out_v[k, x] = plane
    for copy in sent:
        copy.wait_send()


def store(a_in, b_in, a_out, b_out, sems):
    copies = [
        pltpu.make_async_copy(a_in, a_out, sems.at[0]),
        pltpu.make_async_copy(b_in, b_out, sems.at[1]),
    ]
    for copy in copies:
        copy.start()
    for copy in copies:
        copy.wait()


def body(n_gx, n_gz, populations, solid, cell_index, offset, velocity, mass, counts):
    depth_x, ny, nz = populations.shape[1:]
    slots = cell_index.shape[0]
    rows = (slots // nz, nz)
    nzs = 1 if n_gz == 2 else 2
    f32, vmem, dma = jnp.float32, pltpu.VMEM, pltpu.SemaphoreType.DMA
    shapes = (
        jax.ShapeDtypeStruct(populations.shape, f32),
        jax.ShapeDtypeStruct(velocity.shape, f32),
    )
    held = pl.pallas_call(
        functools.partial(kernel, n_gx, n_gz),
        out_shape=shapes,
        in_specs=[pl.BlockSpec(memory_space=pltpu.HBM)] * 6
        + [pl.BlockSpec(memory_space=pl.ANY)],
        out_specs=[pl.BlockSpec(memory_space=pltpu.VMEM)] * 2,
        scratch_shapes=[
            vmem(populations.shape, f32),
            vmem(solid.shape, jnp.int32),
            vmem(rows, jnp.int32),
            vmem(rows, f32),
            vmem(velocity.shape, f32),
            vmem(rows, f32),
            vmem((1, 1), jnp.int32),
            vmem((2 * nz, slots), jnp.bfloat16),
            vmem((18 * ny, slots), jnp.bfloat16),
            *[vmem((n, ny, nz), f32) for n in (6, 6, 8, 8, 9, 9, 3, 3, 5, 5, 5, 5, 2)],
            vmem((2, nzs, 3, ny, nz), f32),
            dma((7,)),
            dma((4,)),
            dma((4,)),
            dma((2,)),
            dma((2,)),
            dma((2, nzs, 3)),
            dma((2, nzs, 3)),
        ],
        compiler_params=pltpu.CompilerParams(
            collective_id=0, has_side_effects=True, vmem_limit_bytes=32 * 1024 * 1024
        ),
    )(
        *[
            pltpu.with_memory_space_constraint(value, pltpu.HBM)
            for value in (
                populations,
                solid,
                cell_index.reshape(rows),
                offset.reshape(rows),
                velocity,
                mass.reshape(rows),
            )
        ],
        counts,
    )
    return pl.pallas_call(
        store,
        out_shape=shapes,
        in_specs=[pl.BlockSpec(memory_space=pltpu.VMEM)] * 2,
        out_specs=[pl.BlockSpec(memory_space=pltpu.HBM)] * 2,
        scratch_shapes=[dma((2,))],
        compiler_params=pltpu.CompilerParams(vmem_limit_bytes=2 * 1024 * 1024),
    )(*held)


def solution(mesh):
    return jax.shard_map(
        functools.partial(body, mesh.shape["gx"], mesh.shape["gz"]),
        mesh=mesh,
        in_specs=(
            P(None, "gx", None, "gz"),
            P("gx", None, "gz"),
            P(("gx", "gz")),
            P(("gx", "gz")),
            P(None, ("gx", "gz")),
            P(("gx", "gz")),
            P("gx", "gz"),
        ),
        out_specs=(P(None, "gx", None, "gz"), P(None, ("gx", "gz"))),
        check_vma=False,
    )
```

```python
import functools

import jax
import jax.numpy as jnp
from jax import lax
from jax.experimental import pallas as pl
from jax.experimental.pallas import tpu as pltpu
from jax.sharding import PartitionSpec as P

LATTICE = [
    (0, 0, 0),
    (1, 0, 0),
    (-1, 0, 0),
    (0, 1, 0),
    (0, -1, 0),
    (0, 0, 1),
    (0, 0, -1),
    (1, 1, 0),
    (-1, -1, 0),
    (1, -1, 0),
    (-1, 1, 0),
    (1, 0, 1),
    (-1, 0, -1),
    (1, 0, -1),
    (-1, 0, 1),
    (0, 1, 1),
    (0, -1, -1),
    (0, 1, -1),
    (0, -1, 1),
]
WEIGHTS = [1.0 / 3.0] + [1.0 / 18.0] * 6 + [1.0 / 36.0] * 12
relax_time = 0.6
coupling = 0.5
settle = 0.02
body_force = 0.0001

OPPOSITE = [0] + [k + 1 if k % 2 else k - 1 for k in range(1, 19)]
XP = [k for k in range(19) if LATTICE[k][0] == 1]
XM = [k for k in range(19) if LATTICE[k][0] == -1]
ZP = [k for k in range(19) if LATTICE[k][2] == 1]
ZM = [k for k in range(19) if LATTICE[k][2] == -1]
LANES = {}
for _k in ZP + ZM:
    for _x in range(2):
        LANES[_k, _x] = len(LANES)


def halves(value):
    high = value.astype(jnp.bfloat16).astype(jnp.float32)
    return high, value - high


def total_of(terms):
    while len(terms) > 1:
        terms = [
            terms[i] + terms[i + 1] if i + 1 < len(terms) else terms[i]
            for i in range(0, len(terms), 2)
        ]
    return terms[0]


def moments(f):
    rho = total_of(list(f))
    mom = []
    for d in range(3):
        up = [f[k] for k in range(19) if LATTICE[k][d] == 1]
        down = [f[k] for k in range(19) if LATTICE[k][d] == -1]
        mom.append(total_of(up) - total_of(down))
    return rho, mom


def pair_terms(k, u, scale, base):
    w = WEIGHTS[k]
    along = total_of(
        [u[d] if LATTICE[k][d] == 1 else -u[d] for d in range(3) if LATTICE[k][d]]
    )
    lift = scale * along
    return w * base + (4.5 * w) * (lift * along), (3.0 * w) * lift


def collide(ks, kept, m, inv, scale):
    u = [value * inv for value in m]
    base = scale * (1.0 - 1.5 * (u[0] * u[0] + u[1] * u[1] + u[2] * u[2]))
    out, terms = {}, {}
    for k in ks:
        if k == 0:
            out[0] = kept[0] + WEIGHTS[0] * base
            continue
        first = k if k % 2 else k - 1
        if first not in terms:
            terms[first] = pair_terms(first, u, scale, base)
        even, odd = terms[first]
        out[k] = kept[k] + (even + odd if k == first else even - odd)
    return out


def kernel(
    n_gx, n_gz,
    pops_in, solid_in, idx_in, off_in, vel_in, mass_in, counts_in,
    out_v, nv_v,
    f_v, solid_v, idx_v, off_v, vel_v, mass_v, counts_v,
    onehot_v, coef_v, a1s, a1r, a2s, a2r, b1s, b1r, b2s, b2r,
    xp_send, xm_send, xp_recv, xm_recv, zsend, zrecv,
    in_sem, r_ss, r_rs, x_ss, x_rs, z_ss, z_rs,
):
    gx, gz = lax.axis_index("gx"), lax.axis_index("gz")
    right, left = lax.rem(gx + 1, n_gx), lax.rem(gx + n_gx - 1, n_gx)
    xpos = {-1: left, 0: gx, 1: right}
    zdirs = (1,) if n_gz == 2 else (1, -1)
    zpos = {1: lax.rem(gz + 1, n_gz), -1: lax.rem(gz + n_gz - 1, n_gz), 0: gz}

    loads = [
        pltpu.make_async_copy(src, dst, in_sem.at[i])
        for i, (src, dst) in enumerate(
            [
                (pops_in, f_v),
                (solid_in, solid_v),
                (idx_in, idx_v),
                (off_in, off_v),
                (mass_in, mass_v),
                (vel_in, vel_v),
                (counts_in, counts_v),
            ]
        )
    ]
    for load in loads:
        load.start()

    peers = [(dx, dz) for dz in (0,) + zdirs for dx in (-1, 0, 1) if (dx, dz) != (0, 0)]
    barrier = pltpu.get_barrier_semaphore()
    for dx, dz in peers:
        pl.semaphore_signal(
            barrier,
            inc=1,
            device_id={"gx": xpos[dx], "gz": zpos[dz]},
            device_id_type=pl.DeviceIdType.MESH,
        )

    sent = []

    def send(src, dst, send_sem, recv_sem, dx, dz):
        copy = pltpu.make_async_remote_copy(
            src_ref=src,
            dst_ref=dst,
            send_sem=send_sem,
            recv_sem=recv_sem,
            device_id={"gx": xpos[dx], "gz": zpos[dz]},
            device_id_type=pl.DeviceIdType.MESH,
        )
        copy.start()
        sent.append(copy)
        return copy

    def send_rim(step):
        return [
            send(
                zsend.at[step],
                zrecv.at[step, s, 1 - dx],
                z_ss.at[step, s, 1 - dx],
                z_rs.at[step, s, 1 - dx],
                dx,
                dz,
            )
            for s, dz in enumerate(zdirs)
            for dx in (-1, 1, 0)
        ]

    ny, nz = f_v.shape[2], f_v.shape[3]
    slots = idx_v.shape[0] * idx_v.shape[1]
    zbits, ybits = nz.bit_length() - 1, ny.bit_length() - 1
    lane = lax.broadcasted_iota(jnp.int32, (ny, nz), 1)
    keep = 1.0 - 1.0 / relax_time
    everything = list(range(19))

    def wide(column):
        return jnp.broadcast_to(column, (ny, nz))

    def pack(columns, packed=None, first=0):
        if packed is None:
            packed = jnp.zeros((ny, nz), jnp.float32)
        for at, (tile, edge) in enumerate(columns, first):
            z = nz - 1 if edge == 0 else 0
            packed = jnp.where(lane == at, wide(tile[:, z : z + 1]), packed)
        return packed

    def rim(step, edge, source, at):
        s = 0 if edge == 0 else len(zdirs) - 1
        return wide(zrecv[step, s, source, :, at : at + 1])

    loads[0].wait()
    loads[1].wait()
    f = [f_v[k] for k in range(19)]
    solid = solid_v[...] > 0

    def cells(f):
        rho, mom = moments(f)
        scale = jnp.where(solid, 0.0, rho * (1.0 / relax_time))
        kept = [jnp.where(solid, f[OPPOSITE[k]], keep * f[k]) for k in range(19)]
        return mom, 1.0 / rho, scale, kept

    mom, inv, scale, kept = cells(f)
    v = [m * inv for m in mom]
    a1s[0] = scale[1]
    for i, k in enumerate(XP):
        a1s[1 + i] = kept[k][1]
    for d in range(3):
        b1s[d] = v[d][0]
    b1s[3] = scale[0]
    for i, k in enumerate(XM):
        b1s[4 + i] = kept[k][0]
    pl.semaphore_wait(barrier, len(peers))
    first = [
        send(b1s, b1r, r_ss.at[0], r_rs.at[0], -1, 0),
        send(a1s, a1r, r_ss.at[1], r_rs.at[1], 1, 0),
    ]

    at0, at1, columns = {}, {}, []
    for edge, ks in enumerate((ZP, ZM)):
        at0[edge] = len(columns)
        for tile in [v[d][0] for d in range(3)] + [scale[0]] + [kept[k][0] for k in ks]:
            columns.append((tile, edge))
        at1[edge] = len(columns)
        for tile in [scale[1]] + [kept[k][1] for k in ks]:
            columns.append((tile, edge))
    packed = pack(columns)

    for load in loads[2:]:
        load.wait()

    def row(ref):
        return jnp.concatenate([ref[j : j + 1, :] for j in range(ref.shape[0])], axis=1)

    idx, off, mass = row(idx_v), row(off_v), row(mass_v)
    live = lax.broadcasted_iota(jnp.int32, (1, slots), 1) < counts_v[...]
    live = jnp.where(live, 1.0, 0.0).astype(jnp.float32)
    yidx = (idx >> zbits) & (ny - 1)
    key = ((idx >> (zbits + ybits)) << zbits) | (idx & (nz - 1))
    onehot_v[...] = jnp.where(
        lax.broadcasted_iota(jnp.int32, (2 * nz, slots), 0) == key, 1.0, 0.0
    ).astype(jnp.bfloat16)
    ymask = lax.broadcasted_iota(jnp.int32, (ny, slots), 0) == yidx
    near = 1.0 - off
    weight = (coupling * live) * mass
    wnear, wfar = weight * near, weight * off
    vel = [vel_v[d : d + 1, :] for d in range(3)]
    channels = [wnear * near, wnear * off, wfar * off]
    channels += [wnear * vel[d] for d in range(3)]
    channels += [wfar * vel[d] for d in range(3)]
    n_ch = len(channels)
    for c, channel in enumerate(channels):
        for h, part in enumerate(halves(channel)):
            at = (h * n_ch + c) * ny
            coef_v[at : at + ny, :] = jnp.where(ymask, part, 0.0).astype(jnp.bfloat16)
    sums = lax.dot_general(
        coef_v[...],
        onehot_v[...],
        (((1,), (1,)), ((), ())),
        preferred_element_type=jnp.float32,
    )
    sums = (sums[: n_ch * ny] + sums[n_ch * ny :]) * relax_time

    def moment(c, x):
        return sums[c * ny : (c + 1) * ny, x * nz : (x + 1) * nz]

    a, b, e = [[moment(c, x) for x in range(2)] for c in range(3)]
    part0, part1, spill = [], [], []
    for d in range(3):
        q = [moment(3 + d, x) for x in range(2)]
        r = [moment(6 + d, x) for x in range(2)]
        extra = relax_time * body_force if d == 0 else 0.0
        part0.append(q[0] - a[0] * v[d][0] - b[0] * v[d][1] + extra)
        part1.append(
            (q[1] - a[1] * v[d][1]) + (r[0] - b[0] * v[d][0] - e[0] * v[d][1]) + extra
        )
        spill.append(r[1] - b[1] * v[d][1])
    m0 = [mom[d][0] + part0[d] for d in range(3)]
    m1 = [mom[d][1] + part1[d] for d in range(3)]
    for d in range(3):
        b2s[d] = m0[d]
        a2s[d] = spill[d]
        a2s[4 + d] = m1[d]
    a2s[3] = e[1]
    a2s[7] = b[1]
    late = len(columns)
    late_columns = [
        (tile, edge) for edge in range(2) for tile in m0 + spill + [e[1]] + m1 + [b[1]]
    ]
    zsend[0] = pack(late_columns, packed, late)
    rims_in = send_rim(0)
    first += [
        send(a2s, a2r, r_ss.at[2], r_rs.at[2], 1, 0),
        send(b2s, b2r, r_ss.at[3], r_rs.at[3], -1, 0),
    ]
    for copy in first:
        copy.wait_recv()
    vfront = [b1r[d] for d in range(3)]
    force = [
        jnp.stack(
            [part0[d] + (a2r[d] - a2r[3] * v[d][0]), part1[d] - b[1] * vfront[d]]
        )
        for d in range(3)
    ]

    def inverse(scale):
        return 1.0 / (relax_time * jnp.where(scale > 0.0, scale, 1.0))

    by = collide(everything, kept, [mom[d] + force[d] for d in range(3)], inv, scale)
    before = collide(
        XP,
        {k: a1r[1 + i] for i, k in enumerate(XP)},
        [a2r[4 + d] - a2r[7] * v[d][0] for d in range(3)],
        inverse(a1r[0]),
        a1r[0],
    )
    after = collide(
        XM,
        {k: b1r[4 + i] for i, k in enumerate(XM)},
        [b2r[d] + (spill[d] - e[1] * vfront[d]) for d in range(3)],
        inverse(b1r[3]),
        b1r[3],
    )
    rims = {}
    for copy in rims_in:
        copy.wait_recv()
    for edge, ks in enumerate((ZP, ZM)):
        base = late + 11 * edge
        flow = {s: [rim(0, edge, s, at0[edge] + d) for d in range(3)] for s in (1, 2)}
        drag = {s: [rim(0, edge, s, base + 3 + d) for d in range(4)] for s in (0, 1)}
        for source, x in ((1, 0), (1, 1), (0, 1), (2, 0)):
            want = [k for k in ks if source == 1 or LATTICE[k][0] == 1 - source]
            if x == 0:
                at = at0[edge] + 3
                t = drag[source - 1]
                m = [
                    rim(0, edge, source, base + d) + (t[d] - t[3] * flow[source][d])
                    for d in range(3)
                ]
            else:
                at = at1[edge]
                ahead = rim(0, edge, source, base + 10)
                m = [
                    rim(0, edge, source, base + 7 + d) - ahead * flow[source + 1][d]
                    for d in range(3)
                ]
            cell_scale = rim(0, edge, source, at)
            known = {k: rim(0, edge, source, at + 1 + ks.index(k)) for k in want}
            post = collide(want, known, m, inverse(cell_scale), cell_scale)
            for k in want:
                rims[k, source, x] = post[k]

    def stream(k, by, before, after, column):
        cx, cy, cz = LATTICE[k]
        if cx == 1:
            planes = [(before[k], 0, 1), (by[k][0], 1, 0)]
        elif cx == -1:
            planes = [(by[k][1], 1, 1), (after[k], 2, 0)]
        else:
            planes = [(by[k][0], 1, 0), (by[k][1], 1, 1)]
        done = []
        for plane, source, x in planes:
            if cz:
                plane = pltpu.roll(plane, 1 if cz == 1 else nz - 1, 1)
                plane = jnp.where(
                    lane == (0 if cz == 1 else nz - 1), column(k, source, x), plane
                )
            if cy:
                plane = pltpu.roll(plane, 1 if cy == 1 else ny - 1, 0)
            done.append(plane)
        return done

    f = [
        jnp.stack(stream(k, by, before, after, lambda *key: rims[key])) for k in everything
    ]

    mom, inv, scale, kept = cells(f)
    by = collide(everything, kept, [mom[d] + force[d] for d in range(3)], inv, scale)
    zsend[1] = pack([(by[k][x], 0 if LATTICE[k][2] == 1 else 1) for k, x in LANES])
    rims_in = send_rim(1)
    for i, k in enumerate(XP):
        xp_send[i] = by[k][1]
    for i, k in enumerate(XM):
        xm_send[i] = by[k][0]
    last = [
        send(xp_send, xp_recv, x_ss.at[0], x_rs.at[0], 1, 0),
        send(xm_send, xm_recv, x_ss.at[1], x_rs.at[1], -1, 0),
    ]

    here = [jnp.concatenate([v[d][0], v[d][1]], axis=1) for d in range(3)]
    ahead = [jnp.concatenate([v[d][1], vfront[d]], axis=1) for d in range(3)]
    high, low = halves(jnp.concatenate(here + ahead, axis=0))
    oh = onehot_v[...]
    found = jnp.dot(high.astype(jnp.bfloat16), oh, preferred_element_type=jnp.float32)
    found = found + jnp.dot(low.astype(jnp.bfloat16), oh, preferred_element_type=jnp.float32)
    for d in range(3):
        mix = near * found[d * ny : (d + 1) * ny] + off * found[(3 + d) * ny : (4 + d) * ny]
        flow = jnp.sum(jnp.where(ymask, mix, 0.0), axis=0, keepdims=True)
        new = vel[d] + coupling * live * (flow - vel[d])
        if d == 1:
            new = new - settle * live
        nv_v[d : d + 1, :] = new

    def column(k, source, x):
        return rim(1, 0 if LATTICE[k][2] == 1 else 1, source, LANES[k, x])

    before = {k: xp_recv.at[i] for i, k in enumerate(XP)}
    after = {k: xm_recv.at[i] for i, k in enumerate(XM)}

    def write(ks):
        for k in ks:
            ghosts = [{k: ref[k][...]} if k in ref else {} for ref in (before, after)]
            for x, plane in enumerate(stream(k, by, *ghosts, column)):
                out_v[k, x] = plane

    write([k for k in everything if not LATTICE[k][0] and not LATTICE[k][2]])
    for copy in last:
        copy.wait_recv()
    write([k for k in everything if LATTICE[k][0] and not LATTICE[k][2]])
    for copy in rims_in:
        copy.wait_recv()
    write([k for k in everything if LATTICE[k][2]])
    for copy in sent:
        copy.wait_send()


def store(a_in, b_in, a_out, b_out, sems):
    copies = [
        pltpu.make_async_copy(a_in, a_out, sems.at[0]),
        pltpu.make_async_copy(b_in, b_out, sems.at[1]),
    ]
    for copy in copies:
        copy.start()
    for copy in copies:
        copy.wait()


def body(n_gx, n_gz, populations, solid, cell_index, offset, velocity, mass, counts):
    depth_x, ny, nz = populations.shape[1:]
    slots = cell_index.shape[0]
    rows = (slots // nz, nz)
    nzs = 1 if n_gz == 2 else 2
    f32, vmem, dma = jnp.float32, pltpu.VMEM, pltpu.SemaphoreType.DMA
    shapes = (
        jax.ShapeDtypeStruct(populations.shape, f32),
        jax.ShapeDtypeStruct(velocity.shape, f32),
    )
    held = pl.pallas_call(
        functools.partial(kernel, n_gx, n_gz),
        out_shape=shapes,
        in_specs=[pl.BlockSpec(memory_space=pltpu.HBM)] * 6
        + [pl.BlockSpec(memory_space=pl.ANY)],
        out_specs=[pl.BlockSpec(memory_space=pltpu.VMEM)] * 2,
        scratch_shapes=[
            vmem(populations.shape, f32),
            vmem(solid.shape, jnp.int32),
            vmem(rows, jnp.int32),
            vmem(rows, f32),
            vmem(velocity.shape, f32),
            vmem(rows, f32),
            vmem((1, 1), jnp.int32),
            vmem((2 * nz, slots), jnp.bfloat16),
            vmem((18 * ny, slots), jnp.bfloat16),
            *[vmem((n, ny, nz), f32) for n in (6, 6, 8, 8, 9, 9, 3, 3, 5, 5, 5, 5, 2)],
            vmem((2, nzs, 3, ny, nz), f32),
            dma((7,)),
            dma((4,)),
            dma((4,)),
            dma((2,)),
            dma((2,)),
            dma((2, nzs, 3)),
            dma((2, nzs, 3)),
        ],
        compiler_params=pltpu.CompilerParams(
            collective_id=0, has_side_effects=True, vmem_limit_bytes=32 * 1024 * 1024
        ),
    )(
        *[
            pltpu.with_memory_space_constraint(value, pltpu.HBM)
            for value in (
                populations,
                solid,
                cell_index.reshape(rows),
                offset.reshape(rows),
                velocity,
                mass.reshape(rows),
            )
        ],
        counts,
    )
    return pl.pallas_call(
        store,
        out_shape=shapes,
        in_specs=[pl.BlockSpec(memory_space=pltpu.VMEM)] * 2,
        out_specs=[pl.BlockSpec(memory_space=pltpu.HBM)] * 2,
        scratch_shapes=[dma((2,))],
        compiler_params=pltpu.CompilerParams(vmem_limit_bytes=2 * 1024 * 1024),
    )(*held)


def solution(mesh):
    return jax.shard_map(
        functools.partial(body, mesh.shape["gx"], mesh.shape["gz"]),
        mesh=mesh,
        in_specs=(
            P(None, "gx", None, "gz"),
            P("gx", None, "gz"),
            P(("gx", "gz")),
            P(("gx", "gz")),
            P(None, ("gx", "gz")),
            P(("gx", "gz")),
            P("gx", "gz"),
        ),
        out_specs=(P(None, "gx", None, "gz"), P(None, ("gx", "gz"))),
        check_vma=False,
    )
```
